32 devices in a mesh: expert: 8 (over z, x), mp: 4 (over y, core).
Axes of the slice: x: 2, y: 2, z: 4, core: 2. Of those that a mesh axis runs over, the one named last changes fastest.
Arguments:
- tokens: bfloat16 [2048, 768], P('expert', 'mp'), may hold values from -6 to 6
- gain_one: bfloat16 [768], P('mp'), may hold values from 0.5 to 1.5
- gain_two: bfloat16 [768], P('mp'), may hold values from 0.5 to 1.5
- w_query: bfloat16 [768, 768], P(None, 'mp'), may hold values from -0.21875 to 0.21875
- w_key: bfloat16 [768, 768], P(None, 'mp'), may hold values from -0.21875 to 0.21875
- w_value: bfloat16 [768, 768], P(None, 'mp'), may hold values from -0.21875 to 0.21875
- w_out: bfloat16 [768, 768], P('mp'), may hold values from -1.75 to 1.75
- bias_table: bfloat16 [32, 12], P(None, 'mp'), may hold values from -4 to 4
- w_router: bfloat16 [768, 8], P('mp'), may hold values from -0.15625 to 0.15625
- w_in: bfloat16 [8, 768, 3072], P('expert', None, 'mp'), may hold values from -0.21875 to 0.21875
- w_exp_out: bfloat16 [8, 3072, 768], P('expert', 'mp'), may hold values from -2.5 to 2.5
- cotangent: bfloat16 [2048, 768], P('expert', 'mp'), may hold values from -6 to 6
- routes: int32 [2048], P('expert'), may hold values from 0 to 7, as said below
- slot_index: int32 [2048], P('expert'), may hold values from 0 to 35
- bucket: int32 [511], replicated, may hold values from 0 to 31
Outputs:
- mixed: bfloat16 [2048, 768], P('expert', 'mp')
- grad_tokens: float32 [2048, 768], P('expert', 'mp')
- grad_gain_one: float32 [768], P('mp')
- grad_gain_two: float32 [768], P('mp')
- grad_query: float32 [768, 768], P(None, 'mp')
- grad_key: float32 [768, 768], P(None, 'mp')
- grad_value: float32 [768, 768], P(None, 'mp')
- grad_out: float32 [768, 768], P('mp')
- grad_table: float32 [32, 12], P(None, 'mp')
- grad_router: float32 [768, 8], P('mp')
- grad_in: float32 [8, 768, 3072], P('expert', None, 'mp')
- grad_exp_out: float32 [8, 3072, 768], P('expert', 'mp')
The draws below stay inside these ranges and needn't reach their ends.
Inputs may be any that keep to these rules, and one draw needn't show every extreme that they name: Within one sequence no two tokens have the same routes and slot_index. Some experts take 36 tokens from every sequence; slots that no token takes stay empty.
All inputs are finite; a program needn't handle non-finite values.
Results may differ from the reference program's by a relative error of at most 0.017.
Values may be sent and summed in bfloat16 or wider, within the bound.
A program may use at most 128 MiB of HBM per device.

```python
import jax
import jax.numpy as jnp
from jax import lax

D = 768
HEADS = 12
HEAD_DIM = 64
FF = 3072
BUCKETS = 32
TOK_DEV = 256
INNER = 768
EXPERTS = 8
CAP = 36
TOKENS = 2048
N_EXPERT = 8


def place_tokens(key):
    slots_all = EXPERTS * CAP
    order = jax.random.permutation(jax.random.fold_in(key, 11), EXPERTS)
    rank_of = jnp.argsort(order)
    busiest = rank_of < max(1, EXPERTS // 8)
    positions = jnp.arange(slots_all, dtype=jnp.int32)
    is_full = busiest[positions // CAP]

    def one_device(device_key):
        jitter = jax.random.randint(jax.random.fold_in(device_key, 1), (slots_all,), 0, 2 ** 20)
        ranking = jnp.where(is_full, 0, 1 + jitter) * slots_all + positions
        chosen = jnp.argsort(ranking)[:TOK_DEV]
        return jax.random.permutation(jax.random.fold_in(device_key, 2), chosen)
    device_keys = jax.random.split(jax.random.fold_in(key, 12), TOKENS // TOK_DEV)
    return jax.vmap(one_device)(device_keys).reshape(-1).astype(jnp.int32)


def draw_routes(key, part):
    placed = place_tokens(key)
    return (placed // CAP).astype(jnp.int32)


def draw_slot_index(key, part):
    placed = place_tokens(key)
    return (placed % CAP).astype(jnp.int32)


def plant(values, rng, smallest, top_value):
    extent = values.shape
    index_at = [jax.random.randint(jax.random.fold_in(rng, axis), (), 0, extent[axis]) for axis in range(len(extent))]
    values = values.at[tuple(index_at)].set(smallest)
    longest = extent.index(max(extent))
    index_at[longest] = (index_at[longest] + 1) % extent[longest]
    return values.at[tuple(index_at)].set(top_value)


def block_levels(key, shape, cuts, low, top_value):
    loudness, own = 1.0, jax.random.fold_in(key, 6)
    for position, parts in cuts:
        steps = jnp.exp(jax.random.uniform(jax.random.fold_in(own, position), (parts,), jnp.float32, low / len(cuts), top_value / len(cuts)))
        loudness = loudness * jnp.repeat(steps, shape[position] // parts).reshape([-1 if axis == position else 1 for axis in range(len(shape))])
    return loudness


def noise(key, shape, scale, limit, shards=(), kind=jnp.bfloat16):
    array = jax.random.normal(key, shape, jnp.float32) * scale
    if len(shards) > 0:
        array = block_levels(key, shape, shards, -0.22, 0.18) * array
    return jnp.clip(array, min=-limit, max=limit).astype(kind)


def setup_inputs(seed: int = 0) -> dict:
    keys = jax.random.split(jax.random.key(seed), 16)
    return {
        "tokens": noise(keys[0], (TOKENS, D), 1.0, 6.0, ((0, 8), (1, 4))),
        "gain_one": jnp.clip(1.0 + 0.1 * jax.random.normal(keys[1], (D,), jnp.float32), 0.5, 1.5).astype(jnp.bfloat16),
        "gain_two": jnp.clip(1.0 + 0.1 * jax.random.normal(keys[2], (D,), jnp.float32), 0.5, 1.5).astype(jnp.bfloat16),
        "w_query": noise(keys[3], (D, INNER), D ** -0.5, 0.21875, ((1, 4),)),
        "w_key": noise(keys[4], (D, INNER), D ** -0.5, 0.21875, ((1, 4),)),
        "w_value": noise(keys[5], (D, INNER), D ** -0.5, 0.21875, ((1, 4),)),
        "w_out": noise(keys[6], (INNER, D), (max(1, INNER * 4 // TOK_DEV)) ** -0.5, 1.75, ((0, 4),)),
        "bias_table": noise(keys[7], (BUCKETS, HEADS), 1.0, 4.0, ((1, 4),)),
        "w_router": noise(keys[8], (D, EXPERTS), (2 * D) ** -0.5, 0.15625, ((0, 4),)),
        "w_in": noise(keys[9], (EXPERTS, D, FF), D ** -0.5, 0.21875, ((0, 8), (2, 4))),
        "w_exp_out": noise(keys[10], (EXPERTS, FF, D), (1.1 * EXPERTS / FF ** 0.5), 2.5, ((0, 8), (1, 4))),
        "cotangent": noise(keys[11], (TOKENS, D), 1.0, 6.0, ((0, 8), (1, 4))),
        "routes": draw_routes(jax.random.fold_in(keys[15], 71), 0),
        "slot_index": draw_slot_index(jax.random.fold_in(keys[15], 71), 0),
        "bucket": plant(jax.random.randint(keys[14], (2 * TOK_DEV - 1,), 0, BUCKETS), jax.random.fold_in(keys[14], 1), 0, BUCKETS - 1).astype(jnp.int32),
    }


@jax.custom_vjp
def low(v):
    return lax.optimization_barrier(v.astype(jnp.bfloat16)).astype(jnp.float32)

@jax.custom_vjp
def low_back(v):
    return v

def low_keep(v):
    return (low(v), None)

def low_pass(kept, grad):
    return (grad,)

def back_keep(v):
    return (v, None)

def back_low(kept, grad):
    return (low(grad),)
low.defvjp(low_keep, low_pass)
low_back.defvjp(back_keep, back_low)

def dot_high(left, right):
    return jnp.dot(left, right, precision=lax.Precision.HIGHEST)

def rms_scale(values, gain):
    return values * lax.rsqrt(lax.optimization_barrier(jnp.mean(values * values, axis=-1, keepdims=True)) + 1e-06) * gain

def attend(seq_rows, w_query, w_key, w_value, w_out, position_bias):
    length = seq_rows.shape[0]
    queries = low_back(low(dot_high(seq_rows, w_query))).reshape(length, HEADS, HEAD_DIM)
    keys_all = low_back(low(dot_high(seq_rows, w_key))).reshape(length, HEADS, HEAD_DIM)
    values_all = low_back(low(dot_high(seq_rows, w_value))).reshape(length, HEADS, HEAD_DIM)
    scores = jnp.einsum('qhd,khd->hqk', queries, keys_all, precision=lax.Precision.HIGHEST) * HEAD_DIM ** (-0.5)
    scores = low_back(scores + position_bias)
    probs = jax.nn.softmax(scores, axis=-1)
    attended = jnp.einsum('hqk,khd->qhd', low(probs), values_all, precision=lax.Precision.HIGHEST)
    attended = low_back(low(attended.reshape(length, HEADS * HEAD_DIM)))
    return low_back(dot_high(attended, w_out))

def expert_ffn(pieces):
    expert_rows, weight_in, weight_out = pieces
    pre_act = low_back(dot_high(expert_rows, weight_in))
    hidden = low(jax.nn.gelu(pre_act, approximate=True))
    return low_back(low(dot_high(hidden, weight_out)))

def forward(tokens, gain_one, gain_two, w_query, w_key, w_value, w_out, bias_table, w_router, w_in, w_exp_out, routes, slot_index, bucket):
    normed_one = low(rms_scale(tokens, gain_one))
    positions = jnp.arange(TOK_DEV, dtype=jnp.int32)
    lookup = bucket[positions[None, :] - positions[:, None] + (TOK_DEV - 1)]
    position_bias = jnp.transpose(bias_table[lookup], (2, 0, 1))

    def one_sequence(seq_rows):
        return attend(seq_rows, w_query, w_key, w_value, w_out, position_bias)
    attn_sum = lax.map(jax.checkpoint(one_sequence), normed_one.reshape(-1, TOK_DEV, D)).reshape(-1, D)
    resid_one = tokens + attn_sum
    normed_two = low(rms_scale(resid_one, gain_two))
    logits = low_back(dot_high(normed_two, w_router))
    router_probs = jax.nn.softmax(logits, axis=-1)
    gate = jnp.take_along_axis(router_probs, routes[:, None], axis=1)
    owner = jnp.arange(TOKENS, dtype=jnp.int32) // TOK_DEV
    slots_all = EXPERTS * CAP
    target = owner * slots_all + routes * CAP + slot_index
    buffer = jnp.zeros((N_EXPERT * slots_all, D), jnp.float32).at[target].set(normed_two)
    buffer = low_back(buffer)
    by_expert = buffer.reshape(N_EXPERT, EXPERTS, CAP, D).transpose(1, 0, 2, 3).reshape(EXPERTS, N_EXPERT * CAP, D)
    results = lax.map(jax.checkpoint(expert_ffn), (by_expert, w_in, w_exp_out))
    homeward = results.reshape(EXPERTS, N_EXPERT, CAP, D).transpose(1, 0, 2, 3).reshape(-1, D)
    returned = homeward[target]
    return resid_one + gate * returned

def reference(tokens, gain_one, gain_two, w_query, w_key, w_value, w_out, bias_table, w_router, w_in, w_exp_out, cotangent, routes, slot_index, bucket):
    floats = [item.astype(jnp.float32) for item in (tokens, gain_one, gain_two, w_query, w_key, w_value, w_out, bias_table, w_router, w_in, w_exp_out)]

    def wrapped(*inputs):
        return forward(*inputs, routes, slot_index, bucket)
    result, pull_back = jax.vjp(wrapped, *floats)
    grads = pull_back(cotangent.astype(jnp.float32))
    return (result.astype(jnp.bfloat16), grads[0], grads[1], grads[2], grads[3], grads[4], grads[5], grads[6], grads[7], grads[8], grads[9], grads[10])
```

```python
import functools

import jax
import jax.numpy as jnp
from jax import lax
from jax.experimental import pallas as pl
from jax.experimental.pallas import tpu as pltpu
from jax.sharding import PartitionSpec as P

HEAD_DIM = 64
EPSILON = 1e-06
MESH = pl.DeviceIdType.MESH
F32 = jnp.float32
BF16 = jnp.bfloat16


def nn(left, right):
    return lax.dot_general(left, right, (((1,), (0,)), ((), ())), preferred_element_type=F32)


def nt(left, right):
    return lax.dot_general(left, right, (((1,), (1,)), ((), ())), preferred_element_type=F32)


def tn(left, right):
    return lax.dot_general(left, right, (((0,), (0,)), ((), ())), preferred_element_type=F32)


def kernel(
    n_exp,
    cap,
    x_in,
    cot_in,
    small_in,
    wq,
    wk,
    wv,
    wo_in,
    table,
    w_in,
    w_eo,
    routes,
    slots,
    bucket_rev,
    mixed_out,
    gtok_out,
    ggain1_out,
    ggain2_out,
    gq_out,
    gk_out,
    gv_out,
    gout_out,
    gtable_out,
    grouter_out,
    rows_out,
    hidden_out,
    dpre_out,
    x_all,
    cot_all,
    small_all,
    wo_all,
    att_own,
    att_all,
    n1_s,
    r1_s,
    q_s,
    k_s,
    v_s,
    probs_s,
    pair_s,
    disp_s,
    part_s,
    rs_s,
    home_send,
    home_s,
    ret_own,
    ret_all,
    gg2_s,
    grouter_s,
    dres_s,
    dq_s,
    dk_s,
    dv_s,
    dn_send,
    dn_recv,
    s1,
    r1,
    s2,
    r2,
    s3,
    r3,
    s4,
    r4,
    s5,
    r5,
    s6,
    r6,
    s7,
    r7,
    s8,
    r8,
):
    e = lax.axis_index("expert")
    m = lax.axis_index("mp")
    n_mp = 4
    cs, length = x_in.shape
    width = cs * n_mp
    half = width // 2
    rows = n_exp * cap
    heads = cs // HEAD_DIM
    factor = HEAD_DIM ** (-0.5)
    quarter = lax.rem(m, 2) * 2 + m // 2

    barrier = pltpu.get_barrier_semaphore()
    for d in range(1, n_mp):
        pl.semaphore_signal(
            barrier, inc=1, device_id=(e, lax.rem(m + d, n_mp)), device_id_type=MESH
        )

    def greet(d, carry):
        pl.semaphore_signal(
            barrier, inc=1, device_id=(lax.rem(e + d, n_exp), m), device_id_type=MESH
        )
        return carry

    lax.fori_loop(1, n_exp, greet, 0)
    pl.semaphore_wait(barrier, n_mp - 1 + n_exp - 1)

    def to_mp(src, dst, send, recv, d):
        return pltpu.make_async_remote_copy(
            src_ref=src,
            dst_ref=dst,
            send_sem=send,
            recv_sem=recv,
            device_id=(e, lax.rem(m + d, n_mp)),
            device_id_type=MESH,
        )

    def to_expert(src, dst, send, recv, d):
        return pltpu.make_async_remote_copy(
            src_ref=src,
            dst_ref=dst,
            send_sem=send,
            recv_sem=recv,
            device_id=(lax.rem(e + d, n_exp), m),
            device_id_type=MESH,
        )

    own = pl.ds(pl.multiple_of(m * cs, cs), cs)
    gathers = []
    for k, (src, full) in enumerate(
        ((x_in, x_all), (small_in, small_all), (wo_in, wo_all), (cot_in, cot_all))
    ):
        for d in range(1, n_mp):
            copy = to_mp(src, full.at[own], s1.at[k, d], r1.at[k, d], d)
            copy.start()
            gathers.append(copy)
    x_all[own] = x_in[...]
    small_all[own] = small_in[...]
    wo_all[own] = wo_in[...]
    cot_all[own] = cot_in[...]

    buckets = table.shape[0]
    onehot = (
        lax.broadcasted_iota(jnp.int32, (buckets, 2 * length), 0) == bucket_rev[...]
    ).astype(F32)
    table_f = table[...].astype(F32)

    def head_bias(h):
        line = jnp.sum(table_f[:, h : h + 1] * onehot, axis=0, keepdims=True)
        spread = jnp.broadcast_to(line, (length, 2 * length))
        turned = pltpu.roll(spread, length + 1, 1, stride=1, stride_axis=0)
        return turned[:, :length]

    for h in range(heads):
        probs_s[h] = head_bias(h)

    for copy in gathers[:6]:
        copy.wait()
    gain1 = small_all[:, n_exp : n_exp + 1].astype(F32)
    gain2 = small_all[:, n_exp + 1 : n_exp + 2].astype(F32)
    xf = x_all[...].astype(F32)
    inv_one = lax.rsqrt(jnp.sum(xf * xf, axis=0, keepdims=True) / width + EPSILON)
    n1_s[...] = (xf * inv_one * gain1).astype(BF16)
    q_s[...] = tn(wq[...], n1_s[...]).astype(BF16)
    k_s[...] = tn(wk[...], n1_s[...]).astype(BF16)
    v_s[...] = tn(wv[...], n1_s[...]).astype(BF16)
    for h in range(heads):
        hs = pl.ds(h * HEAD_DIM, HEAD_DIM)
        scores = tn(k_s[hs], q_s[hs]) * factor + probs_s[h]
        raised = jnp.exp(scores - jnp.max(scores, axis=0, keepdims=True))
        probs = raised / jnp.sum(raised, axis=0, keepdims=True)
        probs_s[h] = probs
        att_own[hs] = nn(v_s[hs], probs.astype(BF16)).astype(BF16)

    gathers2 = []
    for d in range(1, n_mp):
        copy = to_mp(att_own, att_all.at[own], s2.at[d], r2.at[d], d)
        copy.start()
        gathers2.append(copy)
    att_all[own] = att_own[...]
    for copy in gathers[6:] + gathers2:
        copy.wait()

    resid = x_all[...].astype(F32) + tn(wo_all[...], att_all[...])
    r1_s[...] = resid
    inv_two = lax.rsqrt(jnp.sum(resid * resid, axis=0, keepdims=True) / width + EPSILON)
    n2 = (resid * inv_two * gain2).astype(BF16)
    router = small_all[:, :n_exp]
    logits = tn(router, n2)
    lifted = jnp.exp(logits - jnp.max(logits, axis=0, keepdims=True))
    router_probs = lifted / jnp.sum(lifted, axis=0, keepdims=True)
    picked = (
        lax.broadcasted_iota(jnp.int32, (n_exp, length), 0) == routes[...]
    ).astype(F32)
    gate = jnp.sum(router_probs * picked, axis=0, keepdims=True)
    d_ret = (gate * cot_all[...].astype(F32)).astype(BF16)
    pair_s[0] = n2[:half]
    pair_s[1] = n2[half:]
    pair_s[2] = d_ret[:half]
    pair_s[3] = d_ret[half:]
    target = routes[...] * cap + slots[...]
    place = (lax.broadcasted_iota(jnp.int32, (rows, length), 0) == target).astype(F32).astype(BF16)
    disp_s[...] = nt(place, pair_s[quarter]).astype(BF16).reshape(n_exp, cap, half)

    def dispatch(d):
        return to_expert(
            disp_s.at[lax.rem(e + d, n_exp)],
            rows_out.at[quarter, e],
            s3.at[d],
            r3.at[d],
            d,
        )

    def forward(d, j):
        block = lax.rem(e - d + n_exp, n_exp)
        return to_mp(
            rows_out.at[quarter, block],
            rows_out.at[quarter, block],
            s4.at[j, d],
            r4.at[j, d],
            j,
        )

    def send_loop(d, carry):
        dispatch(d).start()
        return carry

    lax.fori_loop(1, n_exp, send_loop, 0)
    rows_out[quarter, e] = disp_s[e]
    for j in range(1, n_mp):
        forward(0, j).start()

    def pass_loop(d, carry):
        dispatch(d).wait_recv()
        for j in range(1, n_mp):
            forward(d, j).start()
        return carry

    lax.fori_loop(1, n_exp, pass_loop, 0)

    def settle(d, carry):
        for j in range(1, n_mp):
            forward(d, j).wait()
        return carry

    lax.fori_loop(0, n_exp, settle, 0)

    def settle_sends(d, carry):
        dispatch(d).wait_send()
        return carry

    lax.fori_loop(1, n_exp, settle_sends, 0)

    in_a = rows_out[0].reshape(rows, half)
    in_b = rows_out[1].reshape(rows, half)
    pre = nn(in_a, w_in[:half]) + nn(in_b, w_in[half:])
    inner = 0.7978845608 * (pre + 0.044715 * pre * pre * pre)
    bent = jnp.tanh(inner)
    hidden_out[...] = (0.5 * pre * (1.0 + bent)).astype(BF16)
    slope = 0.5 * (1.0 + bent) + 0.5 * pre * (1.0 - bent * bent) * 0.7978845608 * (
        1.0 + 3.0 * 0.044715 * pre * pre
    )
    d_hidden = nt(rows_out[2].reshape(rows, half), w_eo[:, :half]) + nt(
        rows_out[3].reshape(rows, half), w_eo[:, half:]
    )
    dpre_out[...] = (d_hidden * slope).astype(BF16)
    part_s[0] = nn(hidden_out[...], w_eo[:, :half]).astype(BF16)
    part_s[1] = nn(hidden_out[...], w_eo[:, half:]).astype(BF16)
    part_s[2] = nt(dpre_out[...], w_in[:half]).astype(BF16)
    part_s[3] = nt(dpre_out[...], w_in[half:]).astype(BF16)

    sums = []
    for d in range(1, n_mp):
        peer = lax.rem(m + d, n_mp)
        peer_quarter = lax.rem(peer, 2) * 2 + peer // 2
        copy = to_mp(part_s.at[peer_quarter], rs_s.at[d], s5.at[d], r5.at[d], d)
        copy.start()
        sums.append(copy)
    for copy in sums:
        copy.wait()
    total = part_s[quarter].astype(F32)
    for d in range(1, n_mp):
        total = total + rs_s[d].astype(F32)
    home_send[...] = total.astype(BF16).reshape(n_exp, cap, half)

    def homeward(d):
        return to_expert(
            home_send.at[lax.rem(e + d, n_exp)], home_s.at[e], s6.at[d], r6.at[d], d
        )

    def home_start(d, carry):
        homeward(d).start()
        return carry

    def home_wait(d, carry):
        homeward(d).wait()
        return carry

    lax.fori_loop(1, n_exp, home_start, 0)
    home_s[e] = home_send[e]
    lax.fori_loop(1, n_exp, home_wait, 0)
    ret_own[...] = tn(home_s[...].reshape(rows, half), place).astype(BF16)
    spot = pl.ds(pl.multiple_of(quarter * half, half), half)
    backs = []
    for d in range(1, n_mp):
        copy = to_mp(ret_own, ret_all.at[spot], s7.at[d], r7.at[d], d)
        copy.start()
        backs.append(copy)
    ret_all[spot] = ret_own[...]
    for copy in backs:
        copy.wait()

    mixed_out[...] = (r1_s[own] + gate * ret_all[own].astype(F32)).astype(BF16)
    cot_f = cot_all[...].astype(F32)
    d_gate = jnp.sum(cot_f * ret_all[:width].astype(F32), axis=0, keepdims=True)
    d_logits = (d_gate * gate * (picked - router_probs)).astype(BF16)
    resid = r1_s[...]
    hat_two = resid * inv_two
    n2_again = (hat_two * gain2).astype(BF16)
    grouter_s[...] = nt(n2_again, d_logits)
    d_n2 = ret_all[width:].astype(F32) + nn(router, d_logits)
    gg2_s[...] = jnp.sum(d_n2 * hat_two, axis=1, keepdims=True)
    u_two = d_n2 * gain2
    d_resid = cot_f + inv_two * (
        u_two - hat_two * (jnp.sum(u_two * hat_two, axis=0, keepdims=True) / width)
    )
    dres_s[...] = d_resid
    grouter_out[...] = grouter_s[own]
    ggain2_out[...] = gg2_s[own]
    d_attn = d_resid.astype(BF16)
    gout_out[...] = nt(att_own[...], d_attn)
    d_att = nn(wo_in[...], d_attn).astype(BF16)

    flip = (
        lax.broadcasted_iota(jnp.int32, (length, length), 0)
        + lax.broadcasted_iota(jnp.int32, (length, length), 1)
        == length - 1
    ).astype(F32).astype(BF16)
    for h in range(heads):
        hs = pl.ds(h * HEAD_DIM, HEAD_DIM)
        d_h = d_att[h * HEAD_DIM : (h + 1) * HEAD_DIM]
        probs = probs_s[h]
        d_probs = tn(v_s[hs], d_h)
        inner_sum = jnp.sum(d_probs * probs, axis=0, keepdims=True)
        d_scores = (probs * (d_probs - inner_sum)).astype(BF16)
        dq_s[hs] = (nn(k_s[hs], d_scores) * factor).astype(BF16)
        dk_s[hs] = (nt(q_s[hs], d_scores) * factor).astype(BF16)
        dv_s[hs] = nt(d_h, probs.astype(BF16)).astype(BF16)
        flipped = nn(flip, d_scores)
        padded = jnp.concatenate([flipped, jnp.zeros_like(flipped)], axis=1)
        turned = pltpu.roll(padded, 0, 1, stride=1, stride_axis=0)
        line = jnp.sum(turned, axis=0, keepdims=True)
        gtable_out[:, h : h + 1] = jnp.sum(onehot * line, axis=1, keepdims=True)

    d_n1 = nn(wq[...], dq_s[...]) + nn(wk[...], dk_s[...]) + nn(wv[...], dv_s[...])
    xf = x_all[...].astype(F32)
    stat = jnp.sum(d_n1 * gain1 * xf * inv_one, axis=0, keepdims=True)
    for p in range(n_mp):
        dn_send[p, :cs] = d_n1[p * cs : (p + 1) * cs].astype(BF16)
        dn_send[p, cs:] = jnp.broadcast_to(stat, (16, length)).astype(BF16)
    lasts = []
    for d in range(1, n_mp):
        copy = to_mp(
            dn_send.at[lax.rem(m + d, n_mp)], dn_recv.at[d], s8.at[d], r8.at[d], d
        )
        copy.start()
        lasts.append(copy)
    gq_out[...] = nt(n1_s[...], dq_s[...])
    gk_out[...] = nt(n1_s[...], dk_s[...])
    gv_out[...] = nt(n1_s[...], dv_s[...])
    for copy in lasts:
        copy.wait()
    both = dn_send[m].astype(F32)
    for d in range(1, n_mp):
        both = both + dn_recv[d].astype(F32)
    d_own = both[:cs]
    mean_own = both[cs : cs + 1] / width
    hat_one = x_in[...].astype(F32) * inv_one
    gain1_own = small_in[:, n_exp : n_exp + 1].astype(F32)
    gtok_out[...] = dres_s[own] + inv_one * (d_own * gain1_own - hat_one * mean_own)
    ggain1_out[...] = jnp.sum(d_own * hat_one, axis=1, keepdims=True)


def body(
    n_exp,
    tokens,
    gain_one,
    gain_two,
    w_query,
    w_key,
    w_value,
    w_out,
    bias_table,
    w_router,
    w_in,
    w_exp_out,
    cotangent,
    routes,
    slot_index,
    bucket,
):
    length, cs = tokens.shape
    n_mp = 4
    width = cs * n_mp
    half = width // 2
    capacity = max(2, (length * 9 + 8 * n_exp - 1) // (8 * n_exp))
    cap = -(-capacity // 16) * 16
    rows = n_exp * cap
    hid = w_in.shape[2]
    heads = cs // HEAD_DIM
    buckets = bias_table.shape[0]
    small = jnp.concatenate([w_router, gain_one[:, None], gain_two[:, None]], axis=1)
    bucket_rev = jnp.concatenate(
        [bucket[::-1], jnp.full((1,), -1, jnp.int32)]
    )[None, :]
    sds = jax.ShapeDtypeStruct
    vm = pltpu.VMEM
    dma = pltpu.SemaphoreType.DMA
    outs = pl.pallas_call(
        functools.partial(kernel, n_exp, cap),
        out_shape=(
            sds((cs, length), BF16),
            sds((cs, length), F32),
            sds((cs, 1), F32),
            sds((cs, 1), F32),
            sds((width, cs), F32),
            sds((width, cs), F32),
            sds((width, cs), F32),
            sds((cs, width), F32),
            sds((buckets, heads), F32),
            sds((cs, n_exp), F32),
            sds((4, n_exp, cap, half), BF16),
            sds((rows, hid), BF16),
            sds((rows, hid), BF16),
        ),
        in_specs=[pl.BlockSpec(memory_space=vm)] * 13,
        out_specs=tuple([pl.BlockSpec(memory_space=vm)] * 13),
        scratch_shapes=[
            vm((width, length), BF16),
            vm((width, length), BF16),
            vm((width, n_exp + 2), BF16),
            vm((width, width), BF16),
            vm((cs, length), BF16),
            vm((width, length), BF16),
            vm((width, length), BF16),
            vm((width, length), F32),
            vm((cs, length), BF16),
            vm((cs, length), BF16),
            vm((cs, length), BF16),
            vm((heads, length, length), F32),
            vm((4, half, length), BF16),
            vm((n_exp, cap, half), BF16),
            vm((4, rows, half), BF16),
            vm((4, rows, half), BF16),
            vm((n_exp, cap, half), BF16),
            vm((n_exp, cap, half), BF16),
            vm((half, length), BF16),
            vm((4 * half, length), BF16),
            vm((width, 1), F32),
            vm((width, n_exp), F32),
            vm((width, length), F32),
            vm((cs, length), BF16),
            vm((cs, length), BF16),
            vm((cs, length), BF16),
            vm((4, cs + 16, length), BF16),
            vm((4, cs + 16, length), BF16),
            dma((4, 4)),
            dma((4, 4)),
            dma((4,)),
            dma((4,)),
            dma((n_exp,)),
            dma((n_exp,)),
            dma((4, n_exp)),
            dma((4, n_exp)),
            dma((4,)),
            dma((4,)),
            dma((n_exp,)),
            dma((n_exp,)),
            dma((4,)),
            dma((4,)),
            dma((4,)),
            dma((4,)),
        ],
        compiler_params=pltpu.CompilerParams(
            collective_id=0, has_side_effects=True, vmem_limit_bytes=60 * 2**20
        ),
    )(
        tokens.T,
        cotangent.T,
        small,
        w_query,
        w_key,
        w_value,
        w_out,
        bias_table,
        w_in[0],
        w_exp_out[0],
        routes[None, :],
        slot_index[None, :],
        bucket_rev,
    )
    mixed, gtok, gg1, gg2, gq, gk, gv, gout, gtable, grouter, blocks, hidden, d_pre = outs
    flat = blocks.reshape(4, rows, half)
    grad_in = jnp.einsum("hsd,sf->hdf", flat[:2], d_pre, preferred_element_type=F32).reshape(
        width, hid
    )
    d_rows = jnp.concatenate([flat[2], flat[3]], axis=1)
    grad_eo = jnp.einsum("sf,sd->fd", hidden, d_rows, preferred_element_type=F32)
    summed = lax.psum((gq, gk, gv, gout, gtable, grouter, gg1[:, 0], gg2[:, 0]), "expert")
    return (
        mixed.T,
        gtok.T,
        summed[6],
        summed[7],
        summed[0],
        summed[1],
        summed[2],
        summed[3],
        summed[4],
        summed[5],
        grad_in[None],
        grad_eo[None],
    )


def solution(mesh):
    return jax.shard_map(
        functools.partial(body, mesh.shape["expert"]),
        mesh=mesh,
        in_specs=(
            P("expert", "mp"),
            P("mp"),
            P("mp"),
            P(None, "mp"),
            P(None, "mp"),
            P(None, "mp"),
            P("mp", None),
            P(None, "mp"),
            P("mp", None),
            P("expert", None, "mp"),
            P("expert", "mp", None),
            P("expert", "mp"),
            P("expert"),
            P("expert"),
            P(),
        ),
        out_specs=(
            P("expert", "mp"),
            P("expert", "mp"),
            P("mp"),
            P("mp"),
            P(None, "mp"),
            P(None, "mp"),
            P(None, "mp"),
            P("mp", None),
            P(None, "mp"),
            P("mp", None),
            P("expert", None, "mp"),
            P("expert", "mp", None),
        ),
        check_vma=False,
    )
```

```python
import functools

import jax
import jax.numpy as jnp
from jax import lax
from jax.experimental import pallas as pl
from jax.experimental.pallas import tpu as pltpu
from jax.sharding import PartitionSpec as P

HEAD_DIM = 64
EPSILON = 1e-06
MESH = pl.DeviceIdType.MESH
F32 = jnp.float32
BF16 = jnp.bfloat16


def nn(left, right):
    return lax.dot_general(left, right, (((1,), (0,)), ((), ())), preferred_element_type=F32)


def nt(left, right):
    return lax.dot_general(left, right, (((1,), (1,)), ((), ())), preferred_element_type=F32)


def tn(left, right):
    return lax.dot_general(left, right, (((0,), (0,)), ((), ())), preferred_element_type=F32)


def kernel(
    n_exp,
    cap,
    n_x,
    x_in,
    cot_in,
    small_in,
    wq,
    wk,
    wv,
    wo_in,
    table,
    w_in,
    w_eo,
    routes,
    slots,
    bucket_rev,
    mixed_out,
    gtok_out,
    grads_out,
    tiny_out,
    rows_out,
    hidden_out,
    dpre_out,
    x_all,
    cot_all,
    small_all,
    wo_all,
    att_own,
    att_all,
    n1_s,
    r1_s,
    q_s,
    k_s,
    v_s,
    probs_s,
    pair_s,
    disp_s,
    part_s,
    rs_s,
    home_send,
    home_s,
    ret_own,
    ret_all,
    dres_s,
    turn_s,
    dq_s,
    dk_s,
    dv_s,
    rs_b,
    rs_c,
    dn_send,
    dn_recv,
    dn_b,
    dn_c,
    g_send,
    g_x,
    g_part,
    g_z,
    g_all,
    tiny_s,
    tiny_x,
    tiny_b,
    tiny_z,
    s1,
    r1,
    s2,
    r2,
    s3,
    r3,
    s4,
    r4,
    s5,
    r5,
    s6,
    r6,
    s7,
    r7,
    s8,
    r8,
    s9,
    r9,
    s10,
    r10,
):
    e = lax.axis_index("expert")
    m = lax.axis_index("mp")
    n_mp = 4
    cs, length = x_in.shape
    width = cs * n_mp
    half = width // 2
    rows = n_exp * cap
    heads = cs // HEAD_DIM
    factor = HEAD_DIM ** (-0.5)
    fuse = n_exp == 8 and n_x == 2
    core = lax.rem(m, 2)
    side = m // 2
    quarter = core * 2 + side
    sibling = m + 1 - 2 * core
    across = lax.rem(m + 2, n_mp)
    far = sibling + 2 - 4 * (sibling // 2)
    across_quarter = core * 2 + 1 - side
    z = e // n_x
    n_z = n_exp // n_x
    x = lax.rem(e, n_x)

    barrier = pltpu.get_barrier_semaphore()
    for d in range(1, n_mp):
        pl.semaphore_signal(
            barrier, inc=1, device_id=(e, lax.rem(m + d, n_mp)), device_id_type=MESH
        )

    def greet(d, carry):
        pl.semaphore_signal(
            barrier, inc=1, device_id=(lax.rem(e + d, n_exp), m), device_id_type=MESH
        )
        return carry

    lax.fori_loop(1, n_exp, greet, 0)
    pl.semaphore_wait(barrier, n_mp - 1 + n_exp - 1)

    def to_mp(src, dst, send, recv, peer):
        return pltpu.make_async_remote_copy(
            src_ref=src,
            dst_ref=dst,
            send_sem=send,
            recv_sem=recv,
            device_id=(e, peer),
            device_id_type=MESH,
        )

    def spread(src, full, place_of, send, recv):
        near = to_mp(src, full.at[place_of(m)], send.at[1], recv.at[1], sibling)
        over = to_mp(src, full.at[place_of(m)], send.at[2], recv.at[2], across)
        theirs = full.at[place_of(across)]
        relay = to_mp(theirs, theirs, send.at[3], recv.at[3], sibling)
        return over, near, relay

    def begin(trio):
        trio[0].start()
        trio[1].start()

    def pass_on(trio):
        trio[0].wait_recv()
        trio[2].start()

    def finish(trio):
        trio[0].wait_send()
        trio[1].wait()
        trio[2].wait()

    def to_expert(src, dst, send, recv, d):
        return pltpu.make_async_remote_copy(
            src_ref=src,
            dst_ref=dst,
            send_sem=send,
            recv_sem=recv,
            device_id=(lax.rem(e + d, n_exp), m),
            device_id_type=MESH,
        )

    def band(p):
        return pl.ds(pl.multiple_of(p * cs, cs), cs)

    own = band(m)
    small_all[m] = small_in[...]
    trios = [
        spread(x_in, x_all, band, s1.at[0], r1.at[0]),
        spread(small_in, small_all, lambda p: p, s1.at[1], r1.at[1]),
        spread(wo_in, wo_all, band, s1.at[2], r1.at[2]),
        spread(cot_in, cot_all, band, s1.at[3], r1.at[3]),
    ]
    for trio in trios:
        begin(trio)
    x_all[own] = x_in[...]
    wo_all[own] = wo_in[...]
    cot_all[own] = cot_in[...]

    buckets = table.shape[0]
    onehot = (
        lax.broadcasted_iota(jnp.int32, (buckets, 2 * length), 0) == bucket_rev[...]
    ).astype(F32)
    table_f = table[...].astype(F32)

    def head_bias(h):
        line = jnp.sum(table_f[:, h : h + 1] * onehot, axis=0, keepdims=True)
        spread = jnp.broadcast_to(line, (length, 2 * length))
        turned = pltpu.roll(spread, length + 1, 1, stride=1, stride_axis=0)
        return turned[:, :length]

    for h in range(heads):
        probs_s[h] = head_bias(h)

    for trio in trios[:2]:
        pass_on(trio)
    for trio in trios[:2]:
        finish(trio)
    n_small = small_in.shape[0]
    unit = (
        lax.broadcasted_iota(jnp.int32, (n_small, n_small), 0)
        == lax.broadcasted_iota(jnp.int32, (n_small, n_small), 1)
    ).astype(F32).astype(BF16)
    for p in range(n_mp):
        turn_s[p * cs : (p + 1) * cs] = tn(small_all[p], unit)
    gain1 = turn_s[:, n_exp : n_exp + 1]
    gain2 = turn_s[:, n_exp + 1 : n_exp + 2]
    xf = x_all[...].astype(F32)
    inv_one = lax.rsqrt(jnp.sum(xf * xf, axis=0, keepdims=True) / width + EPSILON)
    n1_s[...] = (xf * inv_one * gain1).astype(BF16)
    q_s[...] = nn(wq[...], n1_s[...]).astype(BF16)
    k_s[...] = nn(wk[...], n1_s[...]).astype(BF16)
    v_s[...] = nn(wv[...], n1_s[...]).astype(BF16)
    for h in range(heads):
        hs = pl.ds(h * HEAD_DIM, HEAD_DIM)
        scores = tn(k_s[hs], q_s[hs]) * factor + probs_s[h]
        raised = jnp.exp(scores - jnp.max(scores, axis=0, keepdims=True))
        probs = raised / jnp.sum(raised, axis=0, keepdims=True)
        probs_s[h] = probs
        att_own[hs] = nn(v_s[hs], probs.astype(BF16)).astype(BF16)

    att_trio = spread(att_own, att_all, band, s2, r2)
    for trio in trios[2:]:
        pass_on(trio)
    begin(att_trio)
    att_all[own] = att_own[...]
    pass_on(att_trio)
    for trio in trios[2:] + [att_trio]:
        finish(trio)

    resid = x_all[...].astype(F32) + tn(wo_all[...], att_all[...])
    r1_s[...] = resid
    inv_two = lax.rsqrt(jnp.sum(resid * resid, axis=0, keepdims=True) / width + EPSILON)
    n2 = (resid * inv_two * gain2).astype(BF16)
    router = turn_s[:, :n_exp].astype(BF16)
    logits = tn(router, n2)
    lifted = jnp.exp(logits - jnp.max(logits, axis=0, keepdims=True))
    router_probs = lifted / jnp.sum(lifted, axis=0, keepdims=True)
    picked = (
        lax.broadcasted_iota(jnp.int32, (n_exp, length), 0) == routes[...]
    ).astype(F32)
    gate = jnp.sum(router_probs * picked, axis=0, keepdims=True)
    d_ret = (gate * cot_all[...].astype(F32)).astype(BF16)
    pair_s[0] = n2[:half]
    pair_s[1] = n2[half:]
    pair_s[2] = d_ret[:half]
    pair_s[3] = d_ret[half:]
    target = routes[...] * cap + slots[...]
    place = (lax.broadcasted_iota(jnp.int32, (rows, length), 0) == target).astype(F32).astype(BF16)
    disp_s[...] = nt(place, pair_s[quarter]).astype(BF16).reshape(n_exp, cap, half)

    def dispatch(d):
        return to_expert(
            disp_s.at[lax.rem(e + d, n_exp)],
            rows_out.at[quarter, e],
            s3.at[d],
            r3.at[d],
            d,
        )

    def forward(d):
        block = lax.rem(e - d + n_exp, n_exp)
        mine = rows_out.at[quarter, block]
        theirs = rows_out.at[across_quarter, block]
        return (
            to_mp(mine, mine, s4.at[2, d], r4.at[2, d], across),
            to_mp(mine, mine, s4.at[1, d], r4.at[1, d], sibling),
            to_mp(theirs, theirs, s4.at[3, d], r4.at[3, d], sibling),
        )

    def send_loop(d, carry):
        dispatch(d).start()
        return carry

    lax.fori_loop(1, n_exp, send_loop, 0)
    rows_out[quarter, e] = disp_s[e]
    begin(forward(0))

    def pass_loop(d, carry):
        dispatch(d).wait_recv()
        begin(forward(d))
        return carry

    lax.fori_loop(1, n_exp, pass_loop, 0)

    def relay_loop(d, carry):
        pass_on(forward(d))
        return carry

    lax.fori_loop(0, n_exp, relay_loop, 0)

    def settle(d, carry):
        finish(forward(d))
        return carry

    lax.fori_loop(0, n_exp, settle, 0)

    def settle_sends(d, carry):
        dispatch(d).wait_send()
        return carry

    lax.fori_loop(1, n_exp, settle_sends, 0)

    in_a = rows_out[0].reshape(rows, half)
    in_b = rows_out[1].reshape(rows, half)
    pre = nn(in_a, w_in[:half]) + nn(in_b, w_in[half:])
    inner = 0.7978845608 * (pre + 0.044715 * pre * pre * pre)
    bent = jnp.tanh(inner)
    hidden_out[...] = (0.5 * pre * (1.0 + bent)).astype(BF16)
    slope = 0.5 * (1.0 + bent) + 0.5 * pre * (1.0 - bent * bent) * 0.7978845608 * (
        1.0 + 3.0 * 0.044715 * pre * pre
    )
    d_hidden = nt(rows_out[2].reshape(rows, half), w_eo[:, :half]) + nt(
        rows_out[3].reshape(rows, half), w_eo[:, half:]
    )
    dpre_out[...] = (d_hidden * slope).astype(BF16)
    part_s[0] = nn(hidden_out[...], w_eo[:, :half]).astype(BF16)
    part_s[1] = nn(hidden_out[...], w_eo[:, half:]).astype(BF16)
    part_s[2] = nt(dpre_out[...], w_in[:half]).astype(BF16)
    part_s[3] = nt(dpre_out[...], w_in[half:]).astype(BF16)

    def halve(parts, got, passing, last, send, recv):
        first = to_mp(
            parts.at[pl.ds(2 - 2 * core, 2)], got, send.at[1], recv.at[1], sibling
        )
        second = to_mp(passing, last, send.at[2], recv.at[2], across)
        return first, second

    first, second = halve(part_s, rs_s, rs_b, rs_c, s5, r5)
    first.start()
    first.wait()
    rs_b[...] = (part_s[across_quarter].astype(F32) + rs_s[1 - side].astype(F32)).astype(BF16)
    second.start()
    total = part_s[quarter].astype(F32) + rs_s[side].astype(F32)
    second.wait()
    total = total + rs_c[...].astype(F32)
    home_send[...] = total.astype(BF16).reshape(n_exp, cap, half)

    def homeward(d):
        return to_expert(
            home_send.at[lax.rem(e + d, n_exp)], home_s.at[e], s6.at[d], r6.at[d], d
        )

    def home_start(d, carry):
        homeward(d).start()
        return carry

    def home_wait(d, carry):
        homeward(d).wait()
        return carry

    lax.fori_loop(1, n_exp, home_start, 0)
    home_s[e] = home_send[e]
    lax.fori_loop(1, n_exp, home_wait, 0)
    ret_own[...] = tn(home_s[...].reshape(rows, half), place).astype(BF16)
    def quarter_rows(p):
        q = lax.rem(p, 2) * 2 + p // 2
        return pl.ds(pl.multiple_of(q * half, half), half)

    back_trio = spread(ret_own, ret_all, quarter_rows, s7, r7)
    begin(back_trio)
    ret_all[quarter_rows(m)] = ret_own[...]
    pass_on(back_trio)
    finish(back_trio)

    ones = jnp.ones((8, length), F32).astype(BF16)

    def lane_sums(values):
        high = values.astype(BF16)
        rest = (values - high.astype(F32)).astype(BF16)
        return nt(ones[:, : values.shape[1]], high) + nt(ones[:, : values.shape[1]], rest)

    tiny_s[...] = jnp.zeros_like(tiny_s)
    mixed_out[...] = (r1_s[own] + gate * ret_all[own].astype(F32)).astype(BF16)
    cot_f = cot_all[...].astype(F32)
    d_gate = jnp.sum(cot_f * ret_all[:width].astype(F32), axis=0, keepdims=True)
    d_logits = (d_gate * gate * (picked - router_probs)).astype(BF16)
    resid = r1_s[...]
    hat_two = resid * inv_two
    n2_again = (hat_two * gain2).astype(BF16)
    tiny_s[:n_exp] = nt(d_logits, n2_again)
    d_n2 = ret_all[width:].astype(F32) + nn(router, d_logits)
    tiny_s[n_exp : n_exp + 8] = lane_sums(d_n2 * hat_two)
    u_two = d_n2 * gain2
    d_resid = cot_f + inv_two * (
        u_two - hat_two * (jnp.sum(u_two * hat_two, axis=0, keepdims=True) / width)
    )
    dres_s[...] = d_resid
    d_attn = d_resid.astype(BF16)
    lanes = width // n_x
    n_rows = cs // n_z if fuse else cs
    x_peer = n_x - 1 - x

    def lane_band(k):
        return pl.ds(pl.multiple_of(k * lanes, lanes), lanes)

    def row_band(k):
        return pl.ds(pl.multiple_of(k * n_rows, n_rows), n_rows)

    def remote(src, dst, kind, i, d, where):
        return pltpu.make_async_remote_copy(
            src_ref=src,
            dst_ref=dst,
            send_sem=s9.at[kind, i, d],
            recv_sem=r9.at[kind, i, d],
            device_id=(where, m),
            device_id_type=MESH,
        )

    def to_x(i):
        return remote(
            g_send.at[i, :, lane_band(x_peer)], g_x.at[i], 0, i, 0, z * n_x + x_peer
        )

    def to_z(i, d):
        zp = lax.rem(z + d, n_z)
        return remote(g_part.at[i, row_band(zp)], g_z.at[i, d], 1, i, d, zp * n_x + x)

    def out_z(i, d):
        zp = lax.rem(z + d, n_z)
        spot = g_all.at[i, row_band(z), lane_band(x)]
        return remote(spot, spot, 2, i, d, zp * n_x + x)

    def out_x(i):
        spot = g_all.at[i, :, lane_band(x)]
        return remote(spot, spot, 3, i, 0, z * n_x + x_peer)

    def give(i, value):
        if fuse:
            g_send[i] = value.astype(BF16)
            to_x(i).start()
        else:
            grads_out[i] = value

    def phase_z(i):
        to_x(i).wait()
        g_part[i] = (
            g_send[i, :, lane_band(x)].astype(F32) + g_x[i].astype(F32)
        ).astype(BF16)
        for d in range(1, n_z):
            to_z(i, d).start()

    def phase_sum(i):
        for d in range(1, n_z):
            to_z(i, d).wait()
        value = g_part[i, row_band(z)].astype(F32)
        for d in range(1, n_z):
            value = value + g_z[i, d].astype(F32)
        g_all[i, row_band(z), lane_band(x)] = value.astype(BF16)
        for d in range(1, n_z):
            out_z(i, d).start()

    def phase_x(i):
        for d in range(1, n_z):
            out_z(i, d).wait()
        out_x(i).start()

    def phase_end(i):
        out_x(i).wait()
        grads_out[i] = g_all[i].astype(F32)

    give(3, nt(att_own[...], d_attn))
    d_att = nn(wo_in[...], d_attn).astype(BF16)

    flip = (
        lax.broadcasted_iota(jnp.int32, (length, length), 0)
        + lax.broadcasted_iota(jnp.int32, (length, length), 1)
        == length - 1
    ).astype(F32).astype(BF16)
    for h in range(heads):
        hs = pl.ds(h * HEAD_DIM, HEAD_DIM)
        d_h = d_att[h * HEAD_DIM : (h + 1) * HEAD_DIM]
        probs = probs_s[h]
        d_probs = tn(v_s[hs], d_h)
        inner_sum = jnp.sum(d_probs * probs, axis=0, keepdims=True)
        d_scores = (probs * (d_probs - inner_sum)).astype(BF16)
        dq_s[hs] = (nn(k_s[hs], d_scores) * factor).astype(BF16)
        dk_s[hs] = (nt(q_s[hs], d_scores) * factor).astype(BF16)
        dv_s[hs] = nt(d_h, probs.astype(BF16)).astype(BF16)
        flipped = nn(flip, d_scores)
        padded = jnp.concatenate([flipped, jnp.zeros_like(flipped)], axis=1)
        turned = pltpu.roll(padded, 0, 1, stride=1, stride_axis=0)
        line = jnp.sum(turned, axis=0, keepdims=True)
        line8 = jnp.broadcast_to(line, (8, 2 * length))
        high = line8.astype(BF16)
        rest = (line8 - high.astype(F32)).astype(BF16)
        sums = nt(high, onehot.astype(BF16)) + nt(rest, onehot.astype(BF16))
        tiny_s[n_exp + 16 + h : n_exp + 17 + h, :buckets] = sums[:1]

    give(2, nt(dv_s[...], n1_s[...]))
    if fuse:
        phase_z(3)
    give(1, nt(dk_s[...], n1_s[...]))
    give(0, nt(dq_s[...], n1_s[...]))
    d_n1 = tn(wq[...], dq_s[...]) + tn(wk[...], dk_s[...]) + tn(wv[...], dv_s[...])
    xf = x_all[...].astype(F32)
    stat = jnp.sum(d_n1 * gain1 * xf * inv_one, axis=0, keepdims=True)
    for p in range(n_mp):
        q = (p % 2) * 2 + p // 2
        dn_send[q, :cs] = d_n1[p * cs : (p + 1) * cs].astype(BF16)
        dn_send[q, cs:] = jnp.broadcast_to(stat, (16, length)).astype(BF16)
    first, second = halve(dn_send, dn_recv, dn_b, dn_c, s8, r8)
    first.start()
    if fuse:
        phase_z(2)
    first.wait()
    dn_b[...] = (dn_send[across_quarter].astype(F32) + dn_recv[1 - side].astype(F32)).astype(BF16)
    second.start()
    both = dn_send[quarter].astype(F32) + dn_recv[side].astype(F32)
    if fuse:
        phase_z(1)
        phase_sum(3)
        phase_z(0)
    second.wait()
    both = both + dn_c[...].astype(F32)
    d_own = both[:cs]
    mean_own = both[cs : cs + 1] / width
    hat_one = x_in[...].astype(F32) * inv_one
    gain1_own = turn_s[own, n_exp : n_exp + 1]
    gtok_out[...] = dres_s[own] + inv_one * (d_own * gain1_own - hat_one * mean_own)
    tiny_s[n_exp + 8 : n_exp + 16, :cs] = lane_sums(d_own * hat_one)
    if not fuse:
        tiny_out[...] = tiny_s[...]
        return

    def tiny_copy(src, dst, d, where):
        return pltpu.make_async_remote_copy(
            src_ref=src,
            dst_ref=dst,
            send_sem=s10.at[d],
            recv_sem=r10.at[d],
            device_id=(where, m),
            device_id_type=MESH,
        )

    def tiny_over(d):
        return tiny_copy(tiny_b, tiny_z.at[d], d, lax.rem(z + d, n_z) * n_x + x)

    pair = tiny_copy(tiny_s, tiny_x, 0, z * n_x + x_peer)
    pair.start()
    phase_sum(2)
    phase_sum(1)
    phase_x(3)
    pair.wait()
    tiny_b[...] = tiny_s[...] + tiny_x[...]
    for d in range(1, n_z):
        tiny_over(d).start()
    phase_sum(0)
    for i in (2, 1, 0):
        phase_x(i)
    for d in range(1, n_z):
        tiny_over(d).wait()
    value = tiny_b[...]
    for d in range(1, n_z):
        value = value + tiny_z[d]
    tiny_out[...] = value
    for i in (3, 2, 1, 0):
        phase_end(i)


def body(
    n_exp,
    tokens,
    gain_one,
    gain_two,
    w_query,
    w_key,
    w_value,
    w_out,
    bias_table,
    w_router,
    w_in,
    w_exp_out,
    cotangent,
    routes,
    slot_index,
    bucket,
):
    length, cs = tokens.shape
    n_mp = 4
    width = cs * n_mp
    half = width // 2
    capacity = max(2, (length * 9 + 8 * n_exp - 1) // (8 * n_exp))
    cap = -(-capacity // 16) * 16
    rows = n_exp * cap
    hid = w_in.shape[2]
    heads = cs // HEAD_DIM
    buckets = bias_table.shape[0]
    n_small = -(-(n_exp + 2) // 16) * 16
    small = jnp.concatenate(
        [
            w_router.T,
            gain_one[None],
            gain_two[None],
            jnp.zeros((n_small - n_exp - 2, cs), BF16),
        ]
    )
    n_x = 2
    n_z = max(1, n_exp // n_x) if n_exp == 8 else 1
    n_tiny = n_exp + 24
    bucket_rev = jnp.concatenate(
        [bucket[::-1], jnp.full((1,), -1, jnp.int32)]
    )[None, :]
    sds = jax.ShapeDtypeStruct
    vm = pltpu.VMEM
    dma = pltpu.SemaphoreType.DMA
    outs = pl.pallas_call(
        functools.partial(kernel, n_exp, cap, n_x),
        out_shape=(
            sds((cs, length), BF16),
            sds((cs, length), F32),
            sds((4, cs, width), F32),
            sds((n_tiny, width), F32),
            sds((4, n_exp, cap, half), BF16),
            sds((rows, hid), BF16),
            sds((rows, hid), BF16),
        ),
        in_specs=[pl.BlockSpec(memory_space=vm)] * 13,
        out_specs=tuple([pl.BlockSpec(memory_space=vm)] * 7),
        scratch_shapes=[
            vm((width, length), BF16),
            vm((width, length), BF16),
            vm((4, n_small, cs), BF16),
            vm((width, width), BF16),
            vm((cs, length), BF16),
            vm((width, length), BF16),
            vm((width, length), BF16),
            vm((width, length), F32),
            vm((cs, length), BF16),
            vm((cs, length), BF16),
            vm((cs, length), BF16),
            vm((heads, length, length), F32),
            vm((4, half, length), BF16),
            vm((n_exp, cap, half), BF16),
            vm((4, rows, half), BF16),
            vm((2, rows, half), BF16),
            vm((n_exp, cap, half), BF16),
            vm((n_exp, cap, half), BF16),
            vm((half, length), BF16),
            vm((4 * half, length), BF16),
            vm((width, length), F32),
            vm((width, n_small), F32),
            vm((cs, length), BF16),
            vm((cs, length), BF16),
            vm((cs, length), BF16),
            vm((rows, half), BF16),
            vm((rows, half), BF16),
            vm((4, cs + 16, length), BF16),
            vm((2, cs + 16, length), BF16),
            vm((cs + 16, length), BF16),
            vm((cs + 16, length), BF16),
            vm((4, cs, width), BF16),
            vm((4, cs, half), BF16),
            vm((4, cs, half), BF16),
            vm((4, n_z, cs // n_z, half), BF16),
            vm((4, cs, width), BF16),
            vm((n_tiny, width), F32),
            vm((n_tiny, width), F32),
            vm((n_tiny, width), F32),
            vm((n_z, n_tiny, width), F32),
            dma((4, 4)),
            dma((4, 4)),
            dma((4,)),
            dma((4,)),
            dma((n_exp,)),
            dma((n_exp,)),
            dma((4, n_exp)),
            dma((4, n_exp)),
            dma((4,)),
            dma((4,)),
            dma((n_exp,)),
            dma((n_exp,)),
            dma((4,)),
            dma((4,)),
            dma((4,)),
            dma((4,)),
            dma((4, 4, n_z)),
            dma((4, 4, n_z)),
            dma((n_z,)),
            dma((n_z,)),
        ],
        compiler_params=pltpu.CompilerParams(
            collective_id=0, has_side_effects=True, vmem_limit_bytes=60 * 2**20
        ),
    )(
        tokens.T,
        cotangent.T,
        small,
        w_query.T,
        w_key.T,
        w_value.T,
        w_out,
        bias_table,
        w_in[0],
        w_exp_out[0],
        routes[None, :],
        slot_index[None, :],
        bucket_rev,
    )
    mixed, gtok, grads, tiny, blocks, hidden, d_pre = outs
    flat = blocks.reshape(4, rows, half)
    grad_in = jnp.einsum("hsd,sf->hdf", flat[:2], d_pre, preferred_element_type=F32).reshape(
        width, hid
    )
    d_rows = jnp.concatenate([flat[2], flat[3]], axis=1)
    grad_eo = jnp.einsum("sf,sd->fd", hidden, d_rows, preferred_element_type=F32)
    if n_exp != 8:
        grads, tiny = lax.psum((grads, tiny), "expert")
    first = lax.axis_index("mp") * cs
    shared = lax.dynamic_slice_in_dim(tiny[: n_exp + 1], first, cs, 1)
    return (
        mixed.T,
        gtok.T,
        tiny[n_exp + 8, :cs],
        shared[n_exp],
        grads[0].T,
        grads[1].T,
        grads[2].T,
        grads[3],
        tiny[n_exp + 16 : n_exp + 16 + heads, :buckets].T,
        shared[:n_exp].T,
        grad_in[None],
        grad_eo[None],
    )


def solution(mesh):
    return jax.shard_map(
        functools.partial(body, mesh.shape["expert"]),
        mesh=mesh,
        in_specs=(
            P("expert", "mp"),
            P("mp"),
            P("mp"),
            P(None, "mp"),
            P(None, "mp"),
            P(None, "mp"),
            P("mp", None),
            P(None, "mp"),
            P("mp", None),
            P("expert", None, "mp"),
            P("expert", "mp", None),
            P("expert", "mp"),
            P("expert"),
            P("expert"),
            P(),
        ),
        out_specs=(
            P("expert", "mp"),
            P("expert", "mp"),
            P("mp"),
            P("mp"),
            P(None, "mp"),
            P(None, "mp"),
            P(None, "mp"),
            P("mp", None),
            P(None, "mp"),
            P("mp", None),
            P("expert", None, "mp"),
            P("expert", "mp", None),
        ),
        check_vma=False,
    )
```

```python
import functools

import jax
import jax.numpy as jnp
from jax import lax
from jax.experimental import pallas as pl
from jax.experimental.pallas import tpu as pltpu
from jax.sharding import PartitionSpec as P

HEAD_DIM = 64
EPSILON = 1e-06
MESH = pl.DeviceIdType.MESH
F32 = jnp.float32
BF16 = jnp.bfloat16


def nn(left, right):
    return lax.dot_general(left, right, (((1,), (0,)), ((), ())), preferred_element_type=F32)


def nt(left, right):
    return lax.dot_general(left, right, (((1,), (1,)), ((), ())), preferred_element_type=F32)


def tn(left, right):
    return lax.dot_general(left, right, (((0,), (0,)), ((), ())), preferred_element_type=F32)


def kernel(
    n_exp,
    cap,
    n_x,
    x_in,
    cot_in,
    router_in,
    gain1_in,
    gain2_in,
    wq,
    wk,
    wv,
    wo_in,
    table,
    w_in,
    w_eo,
    routes,
    slots,
    bucket_rev,
    mixed_out,
    gtok_out,
    gq_out,
    gk_out,
    gv_out,
    gout_out,
    tiny_out,
    rows_out,
    hidden_out,
    dpre_out,
    x_all,
    cot_all,
    small_all,
    wo_all,
    att_own,
    att_all,
    n1_s,
    r1_s,
    q_s,
    k_s,
    v_s,
    probs_s,
    pair_s,
    disp_s,
    part_s,
    rs_s,
    home_send,
    home_s,
    ret_own,
    ret_all,
    dres_s,
    turn_s,
    small_f,
    small_in,
    tiny_h,
    dq_s,
    dk_s,
    dv_s,
    rs_b,
    rs_c,
    dn_send,
    dn_recv,
    dn_b,
    dn_c,
    g_send,
    g_x,
    g_part,
    g_z,
    g_all,
    tiny_s,
    tiny_x,
    tiny_b,
    tiny_z,
    s1,
    r1,
    s2,
    r2,
    s3,
    r3,
    s4,
    r4,
    s5,
    r5,
    s6,
    r6,
    s7,
    r7,
    s8,
    r8,
    s9,
    r9,
    s10,
    r10,
):
    e = lax.axis_index("expert")
    m = lax.axis_index("mp")
    n_mp = 4
    cs, length = x_in.shape
    width = cs * n_mp
    half = width // 2
    rows = n_exp * cap
    heads = cs // HEAD_DIM
    factor = HEAD_DIM ** (-0.5)
    fuse = n_exp == 8 and n_x == 2
    core = lax.rem(m, 2)
    side = m // 2
    quarter = core * 2 + side
    sibling = m + 1 - 2 * core
    across = lax.rem(m + 2, n_mp)
    far = sibling + 2 - 4 * (sibling // 2)
    across_quarter = core * 2 + 1 - side
    z = e // n_x
    n_z = n_exp // n_x
    x = lax.rem(e, n_x)

    barrier = pltpu.get_barrier_semaphore()
    for d in range(1, n_mp):
        pl.semaphore_signal(
            barrier, inc=1, device_id=(e, lax.rem(m + d, n_mp)), device_id_type=MESH
        )

    def greet(d, carry):
        pl.semaphore_signal(
            barrier, inc=1, device_id=(lax.rem(e + d, n_exp), m), device_id_type=MESH
        )
        return carry

    lax.fori_loop(1, n_exp, greet, 0)
    pl.semaphore_wait(barrier, n_mp - 1 + n_exp - 1)

    def to_mp(src, dst, send, recv, peer):
        return pltpu.make_async_remote_copy(
            src_ref=src,
            dst_ref=dst,
            send_sem=send,
            recv_sem=recv,
            device_id=(e, peer),
            device_id_type=MESH,
        )

    def spread(src, full, place_of, send, recv):
        near = to_mp(src, full.at[place_of(m)], send.at[1], recv.at[1], sibling)
        over = to_mp(src, full.at[place_of(m)], send.at[2], recv.at[2], across)
        theirs = full.at[place_of(across)]
        relay = to_mp(theirs, theirs, send.at[3], recv.at[3], sibling)
        return over, near, relay

    def begin(trio):
        trio[0].start()
        trio[1].start()

    def pass_on(trio):
        trio[0].wait_recv()
        trio[2].start()

    def finish(trio):
        trio[0].wait_send()
        trio[1].wait()
        trio[2].wait()

    def to_expert(src, dst, send, recv, d):
        return pltpu.make_async_remote_copy(
            src_ref=src,
            dst_ref=dst,
            send_sem=send,
            recv_sem=recv,
            device_id=(lax.rem(e + d, n_exp), m),
            device_id_type=MESH,
        )

    def band(p):
        return pl.ds(pl.multiple_of(p * cs, cs), cs)

    own = band(m)
    grads_out = (gq_out, gk_out, gv_out, gout_out)
    small_f[...] = jnp.zeros_like(small_f)
    small_f[:n_exp] = router_in[...].astype(F32)
    small_f[n_exp : n_exp + 1] = gain1_in[...].astype(F32)
    small_f[n_exp + 1 : n_exp + 2] = gain2_in[...].astype(F32)
    small_in[...] = small_f[...].astype(BF16)
    small_all[m] = small_in[...]
    trios = [
        spread(x_in, x_all, band, s1.at[0], r1.at[0]),
        spread(small_in, small_all, lambda p: p, s1.at[1], r1.at[1]),
        spread(wo_in, wo_all, band, s1.at[2], r1.at[2]),
        spread(cot_in, cot_all, band, s1.at[3], r1.at[3]),
    ]
    for trio in trios[:2]:
        begin(trio)
    x_all[own] = x_in[...]
    wo_all[own] = wo_in[...]
    cot_all[own] = cot_in[...]

    buckets = table.shape[1]
    onehot = (
        lax.broadcasted_iota(jnp.int32, (buckets, 2 * length), 0) == bucket_rev[...]
    ).astype(F32)
    lines = nn(table[...], onehot.astype(BF16))

    def head_bias(h):
        line = lines[h : h + 1]
        spread = jnp.broadcast_to(line, (length, 2 * length))
        turned = pltpu.roll(spread, length + 1, 1, stride=1, stride_axis=0)
        return turned[:, :length]

    for h in range(heads):
        probs_s[h] = head_bias(h)

    for trio in trios[:2]:
        pass_on(trio)
    for trio in trios[2:]:
        begin(trio)
    for trio in trios[:2]:
        finish(trio)
    n_small = small_in.shape[0]
    unit = (
        lax.broadcasted_iota(jnp.int32, (n_small, n_small), 0)
        == lax.broadcasted_iota(jnp.int32, (n_small, n_small), 1)
    ).astype(F32).astype(BF16)
    for p in range(n_mp):
        turn_s[p * cs : (p + 1) * cs] = tn(small_all[p], unit)
    gain1 = turn_s[:, n_exp : n_exp + 1]
    gain2 = turn_s[:, n_exp + 1 : n_exp + 2]
    xf = x_all[...].astype(F32)
    inv_one = lax.rsqrt(jnp.sum(xf * xf, axis=0, keepdims=True) / width + EPSILON)
    n1_s[...] = (xf * inv_one * gain1).astype(BF16)
    q_s[...] = nn(wq[...], n1_s[...]).astype(BF16)
    k_s[...] = nn(wk[...], n1_s[...]).astype(BF16)
    v_s[...] = nn(wv[...], n1_s[...]).astype(BF16)
    for h in range(heads):
        hs = pl.ds(h * HEAD_DIM, HEAD_DIM)
        scores = tn(k_s[hs], q_s[hs]) * factor + probs_s[h]
        raised = jnp.exp(scores - jnp.max(scores, axis=0, keepdims=True))
        probs = raised / jnp.sum(raised, axis=0, keepdims=True)
        probs_s[h] = probs
        att_own[hs] = nn(v_s[hs], probs.astype(BF16)).astype(BF16)

    att_trio = spread(att_own, att_all, band, s2, r2)
    for trio in trios[2:]:
        pass_on(trio)
    begin(att_trio)
    att_all[own] = att_own[...]
    pass_on(att_trio)
    for trio in trios[2:] + [att_trio]:
        finish(trio)

    resid = x_all[...].astype(F32) + tn(wo_all[...], att_all[...])
    r1_s[...] = resid
    inv_two = lax.rsqrt(jnp.sum(resid * resid, axis=0, keepdims=True) / width + EPSILON)
    n2 = (resid * inv_two * gain2).astype(BF16)
    router = turn_s[:, :n_exp].astype(BF16)
    logits = tn(router, n2)
    lifted = jnp.exp(logits - jnp.max(logits, axis=0, keepdims=True))
    router_probs = lifted / jnp.sum(lifted, axis=0, keepdims=True)
    picked = (
        lax.broadcasted_iota(jnp.int32, (n_exp, length), 0) == routes[...]
    ).astype(F32)
    gate = jnp.sum(router_probs * picked, axis=0, keepdims=True)
    d_ret = (gate * cot_all[...].astype(F32)).astype(BF16)
    pair_s[0] = n2[:half]
    pair_s[1] = n2[half:]
    pair_s[2] = d_ret[:half]
    pair_s[3] = d_ret[half:]
    target = routes[...] * cap + slots[...]
    place = (lax.broadcasted_iota(jnp.int32, (rows, length), 0) == target).astype(F32).astype(BF16)
    disp_s[...] = nt(place, pair_s[quarter]).astype(BF16).reshape(n_exp, cap, half)

    def dispatch(d):
        return to_expert(
            disp_s.at[lax.rem(e + d, n_exp)],
            rows_out.at[quarter, e],
            s3.at[d],
            r3.at[d],
            d,
        )

    def forward(d):
        block = lax.rem(e - d + n_exp, n_exp)
        mine = rows_out.at[quarter, block]
        theirs = rows_out.at[across_quarter, block]
        return (
            to_mp(mine, mine, s4.at[2, d], r4.at[2, d], across),
            to_mp(mine, mine, s4.at[1, d], r4.at[1, d], sibling),
            to_mp(theirs, theirs, s4.at[3, d], r4.at[3, d], sibling),
        )

    def send_loop(d, carry):
        dispatch(d).start()
        return carry

    lax.fori_loop(1, n_exp, send_loop, 0)
    rows_out[quarter, e] = disp_s[e]
    begin(forward(0))

    def pass_loop(d, carry):
        dispatch(d).wait_recv()
        begin(forward(d))
        return carry

    lax.fori_loop(1, n_exp, pass_loop, 0)

    def relay_loop(d, carry):
        pass_on(forward(d))
        return carry

    lax.fori_loop(0, n_exp, relay_loop, 0)

    def settle(d, carry):
        finish(forward(d))
        return carry

    lax.fori_loop(0, n_exp, settle, 0)

    def settle_sends(d, carry):
        dispatch(d).wait_send()
        return carry

    lax.fori_loop(1, n_exp, settle_sends, 0)

    in_a = rows_out[0].reshape(rows, half)
    in_b = rows_out[1].reshape(rows, half)
    pre = nn(in_a, w_in[:half]) + nn(in_b, w_in[half:])
    inner = 0.7978845608 * (pre + 0.044715 * pre * pre * pre)
    bent = jnp.tanh(inner)
    hidden_out[...] = (0.5 * pre * (1.0 + bent)).astype(BF16)
    slope = 0.5 * (1.0 + bent) + 0.5 * pre * (1.0 - bent * bent) * 0.7978845608 * (
        1.0 + 3.0 * 0.044715 * pre * pre
    )
    d_hidden = nt(rows_out[2].reshape(rows, half), w_eo[:, :half]) + nt(
        rows_out[3].reshape(rows, half), w_eo[:, half:]
    )
    dpre_out[...] = (d_hidden * slope).astype(BF16)
    part_s[0] = nn(hidden_out[...], w_eo[:, :half]).astype(BF16)
    part_s[1] = nn(hidden_out[...], w_eo[:, half:]).astype(BF16)
    part_s[2] = nt(dpre_out[...], w_in[:half]).astype(BF16)
    part_s[3] = nt(dpre_out[...], w_in[half:]).astype(BF16)

    def halve(parts, got, passing, last, send, recv):
        first = to_mp(
            parts.at[pl.ds(2 - 2 * core, 2)], got, send.at[1], recv.at[1], sibling
        )
        second = to_mp(passing, last, send.at[2], recv.at[2], across)
        return first, second

    first, second = halve(part_s, rs_s, rs_b, rs_c, s5, r5)
    first.start()
    first.wait()
    rs_b[...] = (part_s[across_quarter].astype(F32) + rs_s[1 - side].astype(F32)).astype(BF16)
    second.start()
    total = part_s[quarter].astype(F32) + rs_s[side].astype(F32)
    second.wait()
    total = total + rs_c[...].astype(F32)
    home_send[...] = total.astype(BF16).reshape(n_exp, cap, half)

    def homeward(d):
        return to_expert(
            home_send.at[lax.rem(e + d, n_exp)], home_s.at[e], s6.at[d], r6.at[d], d
        )

    def home_start(d, carry):
        homeward(d).start()
        return carry

    def home_wait(d, carry):
        homeward(d).wait()
        return carry

    lax.fori_loop(1, n_exp, home_start, 0)
    home_s[e] = home_send[e]
    lax.fori_loop(1, n_exp, home_wait, 0)
    ret_own[...] = tn(home_s[...].reshape(rows, half), place).astype(BF16)
    def quarter_rows(p):
        q = lax.rem(p, 2) * 2 + p // 2
        return pl.ds(pl.multiple_of(q * half, half), half)

    back_trio = spread(ret_own, ret_all, quarter_rows, s7, r7)
    begin(back_trio)
    ret_all[quarter_rows(m)] = ret_own[...]
    pass_on(back_trio)
    finish(back_trio)

    ones = jnp.ones((8, length), F32).astype(BF16)

    def lane_sums(values):
        high = values.astype(BF16)
        rest = (values - high.astype(F32)).astype(BF16)
        return nt(ones[:, : values.shape[1]], high) + nt(ones[:, : values.shape[1]], rest)

    tiny_s[...] = jnp.zeros_like(tiny_s)
    mixed_out[...] = (r1_s[own] + gate * ret_all[own].astype(F32)).astype(BF16)
    cot_f = cot_all[...].astype(F32)
    d_gate = jnp.sum(cot_f * ret_all[:width].astype(F32), axis=0, keepdims=True)
    d_logits = (d_gate * gate * (picked - router_probs)).astype(BF16)
    resid = r1_s[...]
    hat_two = resid * inv_two
    n2_again = (hat_two * gain2).astype(BF16)
    tiny_s[:n_exp] = nt(d_logits, n2_again)
    d_n2 = ret_all[width:].astype(F32) + nn(router, d_logits)
    tiny_s[n_exp : n_exp + 1] = lane_sums(d_n2 * hat_two)[:1]
    u_two = d_n2 * gain2
    d_resid = cot_f + inv_two * (
        u_two - hat_two * (jnp.sum(u_two * hat_two, axis=0, keepdims=True) / width)
    )
    dres_s[...] = d_resid
    d_attn = d_resid.astype(BF16)
    lanes = width // n_x
    n_rows = cs // n_z if fuse else cs
    x_peer = n_x - 1 - x

    def lane_band(k):
        return pl.ds(pl.multiple_of(k * lanes, lanes), lanes)

    def row_band(k):
        return pl.ds(pl.multiple_of(k * n_rows, n_rows), n_rows)

    def remote(src, dst, kind, i, d, where):
        return pltpu.make_async_remote_copy(
            src_ref=src,
            dst_ref=dst,
            send_sem=s9.at[kind, i, d],
            recv_sem=r9.at[kind, i, d],
            device_id=(where, m),
            device_id_type=MESH,
        )

    def to_x(i):
        return remote(
            g_send.at[i, :, lane_band(x_peer)], g_x.at[i], 0, i, 0, z * n_x + x_peer
        )

    def to_z(i, d):
        zp = lax.rem(z + d, n_z)
        return remote(g_part.at[i, row_band(zp)], g_z.at[i, d], 1, i, d, zp * n_x + x)

    def out_z(i, d):
        zp = lax.rem(z + d, n_z)
        spot = g_all.at[i, row_band(z), lane_band(x)]
        return remote(spot, spot, 2, i, d, zp * n_x + x)

    def out_x(i):
        spot = g_all.at[i, :, lane_band(x)]
        return remote(spot, spot, 3, i, 0, z * n_x + x_peer)

    def give(i, value):
        if fuse:
            g_send[i] = value.astype(BF16)
            to_x(i).start()
        else:
            grads_out[i][...] = value

    def phase_z(i):
        to_x(i).wait()
        g_part[i] = (
            g_send[i, :, lane_band(x)].astype(F32) + g_x[i].astype(F32)
        ).astype(BF16)
        for d in range(1, n_z):
            to_z(i, d).start()

    def phase_sum(i):
        for d in range(1, n_z):
            to_z(i, d).wait()
        value = g_part[i, row_band(z)].astype(F32)
        for d in range(1, n_z):
            value = value + g_z[i, d].astype(F32)
        g_all[i, row_band(z), lane_band(x)] = value.astype(BF16)
        for d in range(1, n_z):
            out_z(i, d).start()

    def phase_x(i):
        for d in range(1, n_z):
            out_z(i, d).wait()
        out_x(i).start()

    def phase_end(i):
        out_x(i).wait()
        grads_out[i][...] = g_all[i].astype(F32)

    give(3, nt(att_own[...], d_attn))
    d_att = nn(wo_in[...], d_attn).astype(BF16)

    flip = (
        lax.broadcasted_iota(jnp.int32, (length, length), 0)
        + lax.broadcasted_iota(jnp.int32, (length, length), 1)
        == length - 1
    ).astype(F32).astype(BF16)
    for h in range(heads):
        hs = pl.ds(h * HEAD_DIM, HEAD_DIM)
        d_h = d_att[h * HEAD_DIM : (h + 1) * HEAD_DIM]
        probs = probs_s[h]
        d_probs = tn(v_s[hs], d_h)
        inner_sum = jnp.sum(d_probs * probs, axis=0, keepdims=True)
        d_scores = (probs * (d_probs - inner_sum)).astype(BF16)
        dq_s[hs] = (nn(k_s[hs], d_scores) * factor).astype(BF16)
        dk_s[hs] = (nt(q_s[hs], d_scores) * factor).astype(BF16)
        dv_s[hs] = nt(d_h, probs.astype(BF16)).astype(BF16)
        flipped = nn(flip, d_scores)
        padded = jnp.concatenate([flipped, jnp.zeros_like(flipped)], axis=1)
        turned = pltpu.roll(padded, 0, 1, stride=1, stride_axis=0)
        line = jnp.sum(turned, axis=0, keepdims=True)
        line8 = jnp.broadcast_to(line, (8, 2 * length))
        high = line8.astype(BF16)
        rest = (line8 - high.astype(F32)).astype(BF16)
        sums = nt(high, onehot.astype(BF16)) + nt(rest, onehot.astype(BF16))
        tiny_s[n_exp + 2 + h : n_exp + 3 + h, :buckets] = sums[:1]
        if fuse and h == heads - 2:
            phase_z(3)

    give(2, nt(dv_s[...], n1_s[...]))
    give(1, nt(dk_s[...], n1_s[...]))
    if fuse:
        phase_sum(3)
    give(0, nt(dq_s[...], n1_s[...]))
    if fuse:
        phase_z(2)
    d_n1 = tn(wq[...], dq_s[...]) + tn(wk[...], dk_s[...]) + tn(wv[...], dv_s[...])
    xf = x_all[...].astype(F32)
    stat = jnp.sum(d_n1 * gain1 * xf * inv_one, axis=0, keepdims=True)
    for p in range(n_mp):
        q = (p % 2) * 2 + p // 2
        dn_send[q, :cs] = d_n1[p * cs : (p + 1) * cs].astype(BF16)
        dn_send[q, cs:] = jnp.broadcast_to(stat, (16, length)).astype(BF16)
    first, second = halve(dn_send, dn_recv, dn_b, dn_c, s8, r8)
    first.start()
    if fuse:
        phase_z(1)
    first.wait()
    dn_b[...] = (dn_send[across_quarter].astype(F32) + dn_recv[1 - side].astype(F32)).astype(BF16)
    second.start()
    both = dn_send[quarter].astype(F32) + dn_recv[side].astype(F32)
    if fuse:
        phase_x(3)
        phase_z(0)
    second.wait()
    both = both + dn_c[...].astype(F32)
    d_own = both[:cs]
    mean_own = both[cs : cs + 1] / width
    hat_one = x_in[...].astype(F32) * inv_one
    gain1_own = turn_s[own, n_exp : n_exp + 1]
    gtok_out[...] = dres_s[own] + inv_one * (d_own * gain1_own - hat_one * mean_own)
    tiny_s[n_exp + 1 : n_exp + 2, :cs] = lane_sums(d_own * hat_one)[:1]
    if not fuse:
        tiny_out[...] = tiny_s[...]
        return

    def tiny_copy(src, dst, d, where):
        return pltpu.make_async_remote_copy(
            src_ref=src,
            dst_ref=dst,
            send_sem=s10.at[d],
            recv_sem=r10.at[d],
            device_id=(where, m),
            device_id_type=MESH,
        )

    def tiny_over(d):
        return tiny_copy(tiny_b, tiny_z.at[d], d, lax.rem(z + d, n_z) * n_x + x)

    tiny_h[...] = tiny_s[...].astype(BF16)
    pair = tiny_copy(tiny_h, tiny_x, 0, z * n_x + x_peer)
    pair.start()
    phase_sum(2)
    phase_sum(1)
    pair.wait()
    tiny_b[...] = (tiny_s[...] + tiny_x[...].astype(F32)).astype(BF16)
    for d in range(1, n_z):
        tiny_over(d).start()
    phase_x(2)
    phase_sum(0)
    phase_x(1)
    phase_end(3)
    phase_end(2)
    phase_x(0)
    for d in range(1, n_z):
        tiny_over(d).wait()
    value = tiny_b[...].astype(F32)
    for d in range(1, n_z):
        value = value + tiny_z[d].astype(F32)
    tiny_out[...] = value
    for i in (1, 0):
        phase_end(i)


def body(
    n_exp,
    tokens,
    gain_one,
    gain_two,
    w_query,
    w_key,
    w_value,
    w_out,
    bias_table,
    w_router,
    w_in,
    w_exp_out,
    cotangent,
    routes,
    slot_index,
    bucket,
):
    length, cs = tokens.shape
    n_mp = 4
    width = cs * n_mp
    half = width // 2
    capacity = max(2, (length * 9 + 8 * n_exp - 1) // (8 * n_exp))
    cap = -(-capacity // 16) * 16
    rows = n_exp * cap
    hid = w_in.shape[2]
    heads = cs // HEAD_DIM
    buckets = bias_table.shape[0]
    n_small = -(-(n_exp + 2) // 16) * 16
    n_x = 2
    n_z = max(1, n_exp // n_x) if n_exp == 8 else 1
    n_tiny = -(-(n_exp + 2 + heads) // 16) * 16
    bucket_rev = jnp.concatenate(
        [bucket[::-1], jnp.full((1,), -1, jnp.int32)]
    )[None, :]
    sds = jax.ShapeDtypeStruct
    vm = pltpu.VMEM
    dma = pltpu.SemaphoreType.DMA
    outs = pl.pallas_call(
        functools.partial(kernel, n_exp, cap, n_x),
        out_shape=(
            sds((cs, length), BF16),
            sds((cs, length), F32),
            sds((cs, width), F32),
            sds((cs, width), F32),
            sds((cs, width), F32),
            sds((cs, width), F32),
            sds((n_tiny, width), F32),
            sds((4, n_exp, cap, half), BF16),
            sds((rows, hid), BF16),
            sds((rows, hid), BF16),
        ),
        in_specs=[pl.BlockSpec(memory_space=vm)] * 15,
        out_specs=tuple([pl.BlockSpec(memory_space=vm)] * 10),
        scratch_shapes=[
            vm((width, length), BF16),
            vm((width, length), BF16),
            vm((4, n_small, cs), BF16),
            vm((width, width), BF16),
            vm((cs, length), BF16),
            vm((width, length), BF16),
            vm((width, length), BF16),
            vm((width, length), F32),
            vm((cs, length), BF16),
            vm((cs, length), BF16),
            vm((cs, length), BF16),
            vm((heads, length, length), F32),
            vm((4, half, length), BF16),
            vm((n_exp, cap, half), BF16),
            vm((4, rows, half), BF16),
            vm((2, rows, half), BF16),
            vm((n_exp, cap, half), BF16),
            vm((n_exp, cap, half), BF16),
            vm((half, length), BF16),
            vm((4 * half, length), BF16),
            vm((width, length), F32),
            vm((width, n_small), F32),
            vm((n_small, cs), F32),
            vm((n_small, cs), BF16),
            vm((n_tiny, width), BF16),
            vm((cs, length), BF16),
            vm((cs, length), BF16),
            vm((cs, length), BF16),
            vm((rows, half), BF16),
            vm((rows, half), BF16),
            vm((4, cs + 16, length), BF16),
            vm((2, cs + 16, length), BF16),
            vm((cs + 16, length), BF16),
            vm((cs + 16, length), BF16),
            vm((4, cs, width), BF16),
            vm((4, cs, half), BF16),
            vm((4, cs, half), BF16),
            vm((4, n_z, cs // n_z, half), BF16),
            vm((4, cs, width), BF16),
            vm((n_tiny, width), F32),
            vm((n_tiny, width), BF16),
            vm((n_tiny, width), BF16),
            vm((n_z, n_tiny, width), BF16),
            dma((4, 4)),
            dma((4, 4)),
            dma((4,)),
            dma((4,)),
            dma((n_exp,)),
            dma((n_exp,)),
            dma((4, n_exp)),
            dma((4, n_exp)),
            dma((4,)),
            dma((4,)),
            dma((n_exp,)),
            dma((n_exp,)),
            dma((4,)),
            dma((4,)),
            dma((4,)),
            dma((4,)),
            dma((4, 4, n_z)),
            dma((4, 4, n_z)),
            dma((n_z,)),
            dma((n_z,)),
        ],
        compiler_params=pltpu.CompilerParams(
            collective_id=0, has_side_effects=True, vmem_limit_bytes=60 * 2**20
        ),
    )(
        tokens.T,
        cotangent.T,
        w_router.T,
        gain_one[None],
        gain_two[None],
        w_query.T,
        w_key.T,
        w_value.T,
        w_out,
        bias_table.T,
        w_in[0],
        w_exp_out[0],
        routes[None, :],
        slot_index[None, :],
        bucket_rev,
    )
    mixed, gtok, *grads, tiny, blocks, hidden, d_pre = outs
    flat = blocks.reshape(4, rows, half)
    grad_in = jnp.einsum("hsd,sf->hdf", flat[:2], d_pre, preferred_element_type=F32).reshape(
        width, hid
    )
    d_rows = jnp.concatenate([flat[2], flat[3]], axis=1)
    grad_eo = jnp.einsum("sf,sd->fd", hidden, d_rows, preferred_element_type=F32)
    if n_exp != 8:
        grads, tiny = lax.psum((grads, tiny), "expert")
    first = lax.axis_index("mp") * cs
    shared = lax.dynamic_slice_in_dim(tiny[: n_exp + 1], first, cs, 1)
    return (
        mixed.T,
        gtok.T,
        tiny[n_exp + 1, :cs],
        shared[n_exp],
        grads[0].T,
        grads[1].T,
        grads[2].T,
        grads[3],
        tiny[n_exp + 2 : n_exp + 2 + heads, :buckets].T,
        shared[:n_exp].T,
        grad_in[None],
        grad_eo[None],
    )


def solution(mesh):
    return jax.shard_map(
        functools.partial(body, mesh.shape["expert"]),
        mesh=mesh,
        in_specs=(
            P("expert", "mp"),
            P("mp"),
            P("mp"),
            P(None, "mp"),
            P(None, "mp"),
            P(None, "mp"),
            P("mp", None),
            P(None, "mp"),
            P("mp", None),
            P("expert", None, "mp"),
            P("expert", "mp", None),
            P("expert", "mp"),
            P("expert"),
            P("expert"),
            P(),
        ),
        out_specs=(
            P("expert", "mp"),
            P("expert", "mp"),
            P("mp"),
            P("mp"),
            P(None, "mp"),
            P(None, "mp"),
            P(None, "mp"),
            P("mp", None),
            P(None, "mp"),
            P("mp", None),
            P("expert", None, "mp"),
            P("expert", "mp", None),
        ),
        check_vma=False,
    )
```
